32 devices in a mesh: parts: 2 (over y), angle: 4 (over z), slab: 2 (over x), tile: 2 (over core).
Axes of the slice: x: 2, y: 2, z: 4, core: 2. Of those that a mesh axis runs over, the one named last changes fastest.
Arguments:
- measured: float32 [4, 4, 32, 128], P('angle', 'tile', ('parts', 'slab')), parts along dimension 2, may hold values from -6 to 6
- x_start: float32 [16, 32, 128], P(('angle', 'tile'), ('parts', 'slab')), parts along dimension 1, may hold values from -6 to 6
- block_pixel: int32 [4, 64], P('angle', 'tile'), may hold values from 0 to 15
- block_det: int32 [4, 64], P('angle', 'tile'), may hold values from 0 to 1
- block_count: int32 [4, 2], P('angle', 'tile'), may hold values from 8 to 32, as said below
- interp: bfloat16 [4, 64, 128, 128], P('angle', 'tile'), may hold values from -0.1875 to 0.1875
- lift_gain: float32 [64], replicated, may hold values from -4 to 4
- lift_bias: float32 [64], replicated, may hold values from -3 to 3
- conv_in: bfloat16 [4, 27, 32, 64], replicated, may hold values from -0.21875 to 0.21875
- conv_bias: float32 [4, 64], replicated, may hold values from -3 to 3
- conv_out: bfloat16 [4, 64, 32], replicated, may hold values from -0.75 to 0.75
- out_gain: float32 [64], replicated, may hold values from -0.75 to 0.75
Outputs:
- estimate: float32 [16, 32, 128], P(('angle', 'tile'), ('parts', 'slab')), parts along dimension 1
- denoised: float32 [16, 32, 128], P(('angle', 'tile'), ('parts', 'slab')), parts along dimension 1
The draws below stay inside these ranges and needn't reach their ends.
There are 2 independent parts, one for each index of `parts`. The reference program is written for one: setup_inputs(seed, part) draws one part's arguments, and reference() takes and returns one part's arrays. A program takes and returns all parts, laid end to end along the dimension named above; an argument that names none is the same for every part. Nothing has to cross between parts.
Inputs may be any that keep to these rules, and one draw needn't show every extreme that they name: `block_count`: slots of an angle and detector half at or past its count hold no block. Some angle and half has all 32 slots live.
All inputs are finite; a program needn't handle non-finite values.
Results may differ from the reference program's by a relative error of at most 0.015.
Values may be sent and summed in bfloat16 or wider, within the bound.
A program may use at most 64 MiB of HBM per device.

```python
import jax
import jax.numpy as jnp
from jax import lax

HALF_SLOT_COUNT = 32
TILE_WIDTH = 128
DBT = 2
CH = 64
LAYERS = 4
ITERS = 2
VIEW_ANGLES = 4
HALVES = 2
ANGLE_SLOTS = 64
DETB = 4
PX = 16
Z = 16


def draw_block_count(key, part):
    key = jax.random.fold_in(key, 7)
    key_tallies, key_fullest, key_emptiest = jax.random.split(key, 3)
    table_entries = VIEW_ANGLES * HALVES
    smallest_count = max(1, HALF_SLOT_COUNT // 4)
    block_tallies = jax.random.randint(key_tallies, (table_entries,), smallest_count, HALF_SLOT_COUNT + 1)
    most_filled = jax.random.randint(key_fullest, (), 0, table_entries)
    least_filled = (most_filled + 1 + jax.random.randint(key_emptiest, (), 0, table_entries - 1)) % table_entries
    block_tallies = block_tallies.at[most_filled].set(HALF_SLOT_COUNT).at[least_filled].set(smallest_count)
    return block_tallies.reshape(VIEW_ANGLES, HALVES).astype(jnp.int32)


def place_ends(array, key, least, high):
    longest = array.shape.index(max(array.shape))
    spots = []
    for shift in (0, 1):
        where = [jax.random.randint(jax.random.fold_in(key, axis), (), 0, length) for axis, length in enumerate(array.shape)]
        where[longest] = (where[longest] + shift) % array.shape[longest]
        spots.append(tuple(where))
    return array.at[spots[0]].set(least).at[spots[1]].set(high)


def levels(stream_key, shape, pieces, smallest, high):
    def one(axis_at, blocks):
        draws = jax.random.uniform(jax.random.fold_in(jax.random.fold_in(stream_key, 6), axis_at), (blocks,), jnp.float32, smallest / len(pieces), high / len(pieces))
        return jnp.repeat(jnp.exp(draws), shape[axis_at] // blocks).reshape((-1,) + (1,) * (len(shape) - axis_at - 1))

    gain = one(*pieces[0])
    for cut in pieces[1:]:
        gain = gain * one(*cut)
    return gain


def normal_values(key, shape, spread, most, shards=(), held_as=jnp.bfloat16):
    level = levels(key, shape, shards, -0.22, 0.18) if shards else 1.0
    values = jax.random.normal(key, shape, jnp.float32) * spread * level
    return jnp.minimum(jnp.maximum(values, -most), most).astype(held_as)


def setup_inputs(seed: int = 0, part: int = 0) -> dict:
    streams_of = jax.random.split(jax.random.key(seed), 13)
    own_keys = jax.random.split(jax.random.fold_in(streams_of[12], part), 13)
    return {
        "measured": normal_values(own_keys[0], (VIEW_ANGLES, DETB, Z, TILE_WIDTH), 1.0, 6.0, ((0, 4), (1, 2), (2, 2)), jnp.float32),
        "x_start": normal_values(own_keys[1], (PX, Z, TILE_WIDTH), 1.0, 6.0, ((0, 8), (1, 2)), jnp.float32),
        "block_pixel": place_ends(jax.random.randint(streams_of[2], (VIEW_ANGLES, ANGLE_SLOTS), 0, PX), jax.random.fold_in(streams_of[2], 1), 0, PX - 1).astype(jnp.int32),
        "block_det": place_ends(jax.random.randint(streams_of[3], (VIEW_ANGLES, ANGLE_SLOTS), 0, DBT), jax.random.fold_in(streams_of[3], 1), 0, DBT - 1).astype(jnp.int32),
        "block_count": draw_block_count(jax.random.fold_in(streams_of[12], 71), part),
        "interp": normal_values(streams_of[5], (VIEW_ANGLES, ANGLE_SLOTS, TILE_WIDTH, TILE_WIDTH), (TILE_WIDTH * HALF_SLOT_COUNT // 4) ** -0.5, 0.1875, ((0, 4), (1, 2))),
        "lift_gain": normal_values(streams_of[6], (CH,), 1.0, 4.0, (), jnp.float32),
        "lift_bias": normal_values(streams_of[7], (CH,), 0.5, 3.0, (), jnp.float32),
        "conv_in": normal_values(streams_of[8], (LAYERS, 27, CH // 2, CH), (27 * (CH // 2)) ** -0.5, 0.21875),
        "conv_bias": normal_values(streams_of[9], (LAYERS, CH), 0.5, 3.0, (), jnp.float32),
        "conv_out": normal_values(streams_of[10], (LAYERS, CH, CH // 2), CH ** -0.5, 0.75),
        "out_gain": normal_values(streams_of[11], (CH,), CH ** -0.5, 0.75, (), jnp.float32),
    }


STEP = 0.2
RHO = 0.5
HIGH = lax.Precision.HIGHEST


def slot_layout(det_rows, row_of_counts):
    slot_numbers = jnp.arange(ANGLE_SLOTS, dtype=jnp.int32)
    detector_halves = slot_numbers // HALF_SLOT_COUNT
    occupied_slots = ((slot_numbers % HALF_SLOT_COUNT) < row_of_counts[detector_halves]).astype(jnp.float32)
    detector = (detector_halves * DBT + det_rows).astype(jnp.int32)
    return occupied_slots, detector


def project(shown, block_pixel, block_det, block_count, interp):
    def one_angle(packed):
        pixel_rows, det_rows, row_of_counts, blocks = packed
        occupied_slots, detector = slot_layout(det_rows, row_of_counts)
        gathered = jnp.take(shown, pixel_rows, axis=0).astype(jnp.float32)
        contribution = jnp.einsum('szp,spb->szb', gathered, blocks.astype(jnp.float32), precision=HIGH)
        selector = (detector[None, :] == jnp.arange(DETB, dtype=jnp.int32)[:, None]).astype(jnp.float32) * occupied_slots[None, :]
        return jnp.einsum('ds,szb->dzb', selector, contribution, precision=HIGH)

    return lax.map(one_angle, (block_pixel, block_det, block_count, interp))


def backproject(misfit, block_pixel, block_det, block_count, interp):
    def one_angle(carry, packed):
        misfit_angle, pixel_rows, det_rows, row_of_counts, blocks = packed
        occupied_slots, detector = slot_layout(det_rows, row_of_counts)
        misfit_slots = jnp.take(misfit_angle, detector, axis=0).astype(jnp.float32)
        smeared = jnp.einsum('szb,spb->szp', misfit_slots, blocks.astype(jnp.float32), precision=HIGH)
        smeared = smeared * occupied_slots[:, None, None]
        selector = (pixel_rows[None, :] == jnp.arange(PX, dtype=jnp.int32)[:, None]).astype(jnp.float32)
        return carry + jnp.einsum('ps,szq->pzq', selector, smeared, precision=HIGH), None

    start_zero = jnp.zeros((PX, Z, TILE_WIDTH), jnp.float32)
    summed, ignored = lax.scan(one_angle, start_zero, (misfit, block_pixel, block_det, block_count, interp))
    return summed


def denoise(noisy_input, lift_gain, lift_bias, conv_in, conv_bias, conv_out, out_gain):
    half_width = CH // 2
    features = lift_gain[:, None, None, None] * noisy_input[None] + lift_bias[:, None, None, None]
    for layer in range(LAYERS):
        if layer % 2 == 0:
            active, passive = features[:half_width], features[half_width:]
        else:
            passive, active = features[:half_width], features[half_width:]
        active_low = active.astype(jnp.bfloat16)
        kernel = conv_in[layer].reshape(3, 3, 3, half_width, CH).astype(jnp.float32)
        convolved = lax.conv_general_dilated(active_low.astype(jnp.float32)[None], kernel, window_strides=(1, 1, 1), padding=((1, 1), (1, 1), (1, 1)), dimension_numbers=("NCDHW", "DHWIO", "NCDHW"), precision=HIGH)[0]
        inner = jax.nn.silu(convolved + conv_bias[layer][:, None, None, None]).astype(jnp.bfloat16)
        passive = passive + jnp.einsum('cxzy,cd->dxzy', inner.astype(jnp.float32), conv_out[layer].astype(jnp.float32), precision=HIGH)
        if layer % 2 == 0:
            features = jnp.concatenate([active, passive], axis=0)
        else:
            features = jnp.concatenate([passive, active], axis=0)
    return noisy_input + jnp.einsum('c,cxzy->xzy', out_gain, features, precision=HIGH)


def reference(measured, x_start, block_pixel, block_det, block_count, interp, lift_gain, lift_bias, conv_in, conv_bias, conv_out, out_gain):
    estimate = x_start
    denoised = x_start
    scaled_dual = jnp.zeros_like(x_start)
    for iteration in range(ITERS):
        shown = estimate.astype(jnp.bfloat16)
        projected = project(shown, block_pixel, block_det, block_count, interp)
        misfit = (projected - measured).astype(jnp.bfloat16)
        gradient = backproject(misfit, block_pixel, block_det, block_count, interp)
        estimate = estimate - STEP * (gradient + RHO * (estimate - denoised + scaled_dual))
        fresh = denoise(estimate + scaled_dual, lift_gain, lift_bias, conv_in, conv_bias, conv_out, out_gain)
        if iteration + 1 < ITERS:
            scaled_dual = scaled_dual + estimate - fresh
        denoised = fresh
    return estimate, denoised
```

```python
import jax
import jax.numpy as jnp
from jax import lax
from jax.experimental import pallas as pl
from jax.experimental.pallas import tpu as pltpu
from jax.sharding import PartitionSpec as P

ITERS = 2
STEP = 0.2
RHO = 0.5
REACH = 2
F32 = jnp.float32
BF16 = jnp.bfloat16
MESH = pl.DeviceIdType.MESH


def kernel(
    group,
    tiles,
    slabs,
    layers,
    channels,
    pixel_ref,
    det_ref,
    count_ref,
    measured_ref,
    start_ref,
    interp_ref,
    conv_in_ref,
    conv_out_ref,
    columns_ref,
    estimate_ref,
    denoised_ref,
    volume,
    volume_rows,
    lhs,
    smeared,
    partial,
    arrived,
    halo,
    weights,
    weights_out,
    features,
    taps,
    products,
    gather_send,
    gather_recv,
    sum_send,
    sum_recv,
    halo_send,
    halo_recv,
):
    half = channels // 2
    part = lax.axis_index("parts")
    slab = lax.axis_index("slab")
    me = lax.axis_index("angle") * tiles + lax.axis_index("tile")
    slots = interp_ref.shape[0] // 128

    def device(member, at_slab):
        return (part, member // tiles, at_slab, lax.rem(member, tiles))

    offsets = [
        (ds, dg) for ds in (-1, 0, 1) for dg in range(-REACH, REACH + 1) if (ds, dg) != (0, 0)
    ]

    def present(ds, dg):
        return jnp.logical_and(
            jnp.logical_and(me + dg >= 0, me + dg < group),
            jnp.logical_and(slab + ds >= 0, slab + ds < slabs),
        )

    def partners(body):
        def step(k, carry):
            body(lax.rem(me + k, group))
            return carry

        lax.fori_loop(1, group, step, 0)

    def neighbours(body):
        for ds, dg in offsets:
            pl.when(present(ds, dg))(lambda ds=ds, dg=dg: body(ds, dg))

    halo[...] = jnp.zeros_like(halo)

    barrier = pltpu.get_barrier_semaphore()
    partners(
        lambda other: pl.semaphore_signal(
            barrier, inc=1, device_id=device(other, slab), device_id_type=MESH
        )
    )
    greeted = group - 1
    for ds, dg in offsets:
        if ds == 0:
            continue

        def greet(ds=ds, dg=dg):
            pl.semaphore_signal(
                barrier, inc=1, device_id=device(me + dg, slab + ds), device_id_type=MESH
            )

        pl.when(present(ds, dg))(greet)
        greeted = greeted + present(ds, dg).astype(jnp.int32)
    pl.semaphore_wait(barrier, greeted)

    def gather_copy(turn, other, owner):
        return pltpu.make_async_remote_copy(
            src_ref=volume.at[turn, me],
            dst_ref=volume.at[turn, owner],
            send_sem=gather_send.at[turn, other],
            recv_sem=gather_recv.at[turn, owner],
            device_id=device(other, slab),
            device_id_type=MESH,
        )

    def gather_start(turn, block):
        volume[turn, me] = block.astype(BF16)
        partners(lambda other: gather_copy(turn, other, me).start())

    def gather_wait(turn):
        def wait(other):
            gather_copy(turn, other, other).wait_recv()
            gather_copy(turn, other, other).wait_send()

        partners(wait)

    def sum_copy(turn, other, owner):
        return pltpu.make_async_remote_copy(
            src_ref=partial.at[turn, other],
            dst_ref=arrived.at[turn, owner],
            send_sem=sum_send.at[turn, other],
            recv_sem=sum_recv.at[turn, owner],
            device_id=device(other, slab),
            device_id_type=MESH,
        )

    def sum_finish(turn):
        def step(k, total):
            other = lax.rem(me + k, group)
            sum_copy(turn, other, other).wait_recv()
            sum_copy(turn, other, other).wait_send()
            return total + arrived[turn, other]

        return lax.fori_loop(1, group, step, partial[turn, me])

    def halo_copy(turn, ds, dg, send):
        place = (1 - ds) * (2 * REACH + 1) + REACH - dg
        if not send:
            place = (1 + ds) * (2 * REACH + 1) + REACH + dg
        sent_place = (1 + ds) * (2 * REACH + 1) + REACH + dg
        return pltpu.make_async_remote_copy(
            src_ref=halo.at[turn, 3 * REACH + 1],
            dst_ref=halo.at[turn, place],
            send_sem=halo_send.at[turn, sent_place],
            recv_sem=halo_recv.at[turn, place],
            device_id=device(me + dg, slab + ds),
            device_id_type=MESH,
        )

    def halo_start(turn, block):
        halo[turn, 3 * REACH + 1] = block
        neighbours(lambda ds, dg: halo_copy(turn, ds, dg, True).start())

    def halo_wait(turn):
        def wait(ds, dg):
            halo_copy(turn, ds, dg, False).wait_recv()
            halo_copy(turn, ds, dg, False).wait_send()

        neighbours(wait)

    def data_step(turn):
        def widen(member, carry):
            volume_rows[pl.ds(2 * member, 2)] = (
                volume[turn, member].astype(F32).reshape(2, 8, 128)
            )
            return carry

        lax.fori_loop(0, group, widen, 0)
        live = [(count_ref[0, 0] > s).astype(F32) for s in range(slots)]
        first = [
            jnp.where(det_ref[0, s] == 0, F32(1.0), F32(0.0)) * live[s] for s in range(slots)
        ]
        second = [
            jnp.where(det_ref[0, s] == 1, F32(1.0), F32(0.0)) * live[s] for s in range(slots)
        ]
        for s in range(slots):
            row = volume_rows[pixel_ref[0, s]]
            lhs[:, 128 * s : 128 * (s + 1)] = jnp.concatenate(
                [row * first[s], row * second[s]], axis=0
            ).astype(BF16)
        projected = jnp.dot(lhs[...], interp_ref[...], preferred_element_type=F32)
        misfit = (projected - measured_ref[...]).astype(BF16)
        for s in range(0, slots, 2):
            both = lax.dot_general(
                misfit,
                interp_ref[128 * s : 128 * (s + 2), :],
                (((1,), (1,)), ((), ())),
                preferred_element_type=F32,
            )
            for k in range(2):
                block = both[:, 128 * k : 128 * (k + 1)]
                smeared[s + k] = block[:8] * first[s + k] + block[8:] * second[s + k]

        def rows_of(owner, carry):
            totals = [jnp.zeros((8, 128), F32) for _ in range(8)]
            for s in range(slots):
                at = jnp.full((8, 128), pixel_ref[0, s], jnp.int32) - 8 * owner
                block = smeared[s]
                for k in range(8):
                    totals[k] = totals[k] + jnp.where(at == k, block, 0.0)
            for k in range(4):
                partial[turn, 4 * owner + k] = jnp.concatenate(
                    totals[2 * k : 2 * k + 2], axis=0
                )
            return carry

        lax.fori_loop(0, group // 4, rows_of, 0)
        partners(lambda other: sum_copy(turn, other, me).start())

    def prepare_weights():
        for layer in range(layers):
            for oz in range(3):
                stacked = jnp.concatenate(
                    [
                        conv_in_ref[layer, 9 * ox + 3 * oz + oy]
                        for ox in range(3)
                        for oy in range(3)
                    ],
                    axis=0,
                )
                weights[layer, channels * oz : channels * (oz + 1), :] = (
                    stacked.astype(F32).T.astype(BF16)
                )
            weights_out[layer] = conv_out_ref[layer].astype(F32).T.astype(BF16)

    def column(index):
        return columns_ref[channels * index : channels * (index + 1), :]

    rows = 2 + 4 * REACH
    depth = 8 + 2 * layers
    lanes = lax.broadcasted_iota(jnp.int32, (half, 128), 1)

    def denoise(turn):
        gain, bias = column(0), column(1)

        def lift(i, carry):
            block, low = i // 2, 8 * lax.rem(i, 2)
            above = halo[turn, block, pl.ds(pl.multiple_of(low, 8), 8), :]
            here = halo[turn, 2 * REACH + 1 + block, pl.ds(pl.multiple_of(low, 8), 8), :]
            below = halo[turn, 4 * REACH + 2 + block, pl.ds(pl.multiple_of(low, 8), 8), :]
            line = jnp.concatenate([above[8 - layers :], here, below[:layers]], axis=0)
            for j in range(depth):
                features[i, j] = gain * line[j : j + 1, :] + bias
            return carry

        lax.fori_loop(0, rows, lift, 0)

        for layer in range(layers):
            active, passive = (0, half) if layer % 2 == 0 else (half, 0)

            def spread(i, carry):
                row = 2 * me - 2 * REACH + i
                row_in = jnp.logical_and(row >= 0, row < 2 * group)
                for j in range(layer, depth - layer):
                    at = 8 * slab - layers + j
                    inside = jnp.logical_and(row_in, jnp.logical_and(at >= 0, at < 8 * slabs))
                    block = features[i, j, active : active + half, :] * inside.astype(F32)
                    before = jnp.where(lanes == 0, 0.0, pltpu.roll(block, 1, 1))
                    after = jnp.where(lanes == 127, 0.0, pltpu.roll(block, 127, 1))
                    taps[j, i] = jnp.concatenate([before, block, after], axis=0).astype(BF16)
                return carry

            lax.fori_loop(layer, rows - layer, spread, 0)
            bias_wide = jnp.concatenate([column(3 + layer)] * 2, axis=1)

            def multiply(r, j):
                left = taps[j, pl.ds(r - 1, 3)].reshape(9 * half, 128)
                right = taps[j, pl.ds(r, 3)].reshape(9 * half, 128)
                products[j] = jnp.dot(
                    weights[layer],
                    jnp.concatenate([left, right], axis=1),
                    preferred_element_type=F32,
                )

            def finish(r, j):
                total = (
                    products[j - 1, :channels]
                    + products[j, channels : 2 * channels]
                    + products[j + 1, 2 * channels :]
                    + bias_wide
                )
                inner = (total / (1.0 + jnp.exp(-total))).astype(BF16)
                change = jnp.dot(weights_out[layer], inner, preferred_element_type=F32)
                features[r, j, passive : passive + half, :] += change[:, :128]
                features[r + 1, j, passive : passive + half, :] += change[:, 128:]

            def pair(index, carry):
                r = layer + 1 + 2 * index
                low, high = layer + 1, depth - layer - 1
                for j in (low - 1, low, low + 1):
                    multiply(r, j)

                def along(j, carry):
                    finish(r, j - 2)
                    multiply(r, j)
                    return carry

                lax.fori_loop(low + 2, high + 1, along, 0)
                finish(r, high - 1)
                return carry

            lax.fori_loop(0, rows // 2 - 1 - layer, pair, 0)

        readout = column(2)
        lines = []
        for i in range(2):
            for j in range(8):
                lines.append(
                    jnp.sum(
                        features[2 * REACH + i, layers + j] * readout, axis=0, keepdims=True
                    )
                )
        return halo[turn, 3 * REACH + 1] + jnp.concatenate(lines, axis=0)

    estimate = start_ref[...]
    denoised = estimate
    scaled_dual = jnp.zeros_like(estimate)
    gather_start(0, estimate)
    prepare_weights()
    gather_wait(0)
    data_step(0)
    for turn in range(ITERS):
        gradient = sum_finish(turn)
        estimate = estimate - STEP * (gradient + RHO * (estimate - denoised + scaled_dual))
        if turn + 1 == ITERS:
            estimate_ref[...] = estimate
        halo_start(turn, estimate + scaled_dual)
        if turn + 1 < ITERS:
            gather_start(turn + 1, estimate)
            gather_wait(turn + 1)
            data_step(turn + 1)
        halo_wait(turn)
        fresh = denoise(turn)
        if turn + 1 < ITERS:
            scaled_dual = scaled_dual + estimate - fresh
        denoised = fresh
    denoised_ref[...] = denoised


def solution(mesh):
    in_specs = (
        P("angle", "tile", ("parts", "slab"), None),
        P(("angle", "tile"), ("parts", "slab"), None),
        P("angle", "tile"),
        P("angle", "tile"),
        P("angle", "tile"),
        P("angle", "tile", None, None),
        P(),
        P(),
        P(),
        P(),
        P(),
        P(),
    )
    out_specs = (
        P(("angle", "tile"), ("parts", "slab"), None),
        P(("angle", "tile"), ("parts", "slab"), None),
    )
    tiles = mesh.shape["tile"]
    group = mesh.shape["angle"] * tiles
    slabs = mesh.shape["slab"]

    def local(
        measured,
        x_start,
        block_pixel,
        block_det,
        block_count,
        interp,
        lift_gain,
        lift_bias,
        conv_in,
        conv_bias,
        conv_out,
        out_gain,
    ):
        channels = lift_gain.shape[0]
        layers = conv_in.shape[0]
        slots = interp.shape[1]
        half = channels // 2
        rows, depth = 2 + 4 * REACH, 8 + 2 * layers
        columns = jnp.concatenate([lift_gain, lift_bias, out_gain, conv_bias.reshape(-1)])
        columns = jnp.broadcast_to(columns[:, None], (columns.shape[0], 128))
        vmem = pl.BlockSpec(memory_space=pltpu.VMEM)
        smem = pl.BlockSpec(memory_space=pltpu.SMEM)
        places = 3 * (2 * REACH + 1)

        def run(*refs):
            kernel(group, tiles, slabs, layers, channels, *refs)

        estimate, denoised = pl.pallas_call(
            run,
            out_shape=[jax.ShapeDtypeStruct((16, 128), F32)] * 2,
            in_specs=[smem] * 3 + [vmem] * 6,
            out_specs=[vmem] * 2,
            scratch_shapes=[
                pltpu.VMEM((ITERS, group, 16, 128), BF16),
                pltpu.VMEM((2 * group, 8, 128), F32),
                pltpu.VMEM((16, 128 * slots), BF16),
                pltpu.VMEM((slots, 8, 128), F32),
                pltpu.VMEM((ITERS, group, 16, 128), F32),
                pltpu.VMEM((ITERS, group, 16, 128), F32),
                pltpu.VMEM((ITERS, places, 16, 128), F32),
                pltpu.VMEM((layers, 3 * channels, 9 * half), BF16),
                pltpu.VMEM((layers, half, channels), BF16),
                pltpu.VMEM((rows, depth, channels, 128), F32),
                pltpu.VMEM((depth, rows, 3 * half, 128), BF16),
                pltpu.VMEM((depth, 3 * channels, 256), F32),
                pltpu.SemaphoreType.DMA((ITERS, group)),
                pltpu.SemaphoreType.DMA((ITERS, group)),
                pltpu.SemaphoreType.DMA((ITERS, group)),
                pltpu.SemaphoreType.DMA((ITERS, group)),
                pltpu.SemaphoreType.DMA((ITERS, places)),
                pltpu.SemaphoreType.DMA((ITERS, places)),
            ],
            compiler_params=pltpu.CompilerParams(
                collective_id=0, has_side_effects=True, vmem_limit_bytes=48 * 1024 * 1024
            ),
        )(
            block_pixel,
            block_det,
            block_count,
            measured.reshape(16, 128),
            x_start.reshape(16, 128),
            interp.reshape(slots * 128, 128),
            conv_in,
            conv_out,
            columns,
        )
        return estimate.reshape(2, 8, 128), denoised.reshape(2, 8, 128)

    return jax.shard_map(local, mesh=mesh, in_specs=in_specs, out_specs=out_specs, check_vma=False)
```

```python
import jax
import jax.numpy as jnp
from jax import lax
from jax.experimental import pallas as pl
from jax.experimental.pallas import tpu as pltpu
from jax.sharding import PartitionSpec as P

ITERS = 2
STEP = 0.2
RHO = 0.5
REACH = 2
F32 = jnp.float32
BF16 = jnp.bfloat16
MESH = pl.DeviceIdType.MESH


def kernel(
    group,
    tiles,
    slabs,
    layers,
    channels,
    pixel_in,
    det_in,
    count_in,
    start_in,
    measured_in,
    interp_in,
    conv_in_in,
    conv_out_in,
    gain_in,
    bias_in,
    readout_in,
    conv_bias_in,
    estimate_ref,
    denoised_ref,
    pixel_ref,
    det_ref,
    count_ref,
    start_ref,
    measured_ref,
    interp_ref,
    conv_in_ref,
    conv_out_ref,
    gain_ref,
    bias_ref,
    readout_ref,
    conv_bias_ref,
    columns_ref,
    volume,
    volume_rows,
    lhs,
    smeared,
    partial,
    arrived,
    halo,
    weights,
    weights_out,
    features,
    taps_even,
    taps_odd,
    products,
    input_sems,
    gather_send,
    gather_recv,
    sum_send,
    sum_recv,
    halo_send,
    halo_recv,
):
    half = channels // 2
    part = lax.axis_index("parts")
    slab = lax.axis_index("slab")
    me = lax.axis_index("angle") * tiles + lax.axis_index("tile")
    slots = interp_ref.shape[0] // 128

    def device(member, at_slab):
        return (part, member // tiles, at_slab, lax.rem(member, tiles))

    offsets = [
        (ds, dg) for ds in (-1, 0, 1) for dg in range(-REACH, REACH + 1) if (ds, dg) != (0, 0)
    ]

    def present(ds, dg):
        return jnp.logical_and(
            jnp.logical_and(me + dg >= 0, me + dg < group),
            jnp.logical_and(slab + ds >= 0, slab + ds < slabs),
        )

    def partners(body):
        def step(k, carry):
            body(lax.rem(me + k, group))
            return carry

        lax.fori_loop(1, group, step, 0)

    def neighbours(body):
        for ds, dg in offsets:
            pl.when(present(ds, dg))(lambda ds=ds, dg=dg: body(ds, dg))

    loads = [
        pltpu.make_async_copy(source, target, input_sems.at[index])
        for index, (source, target) in enumerate(
            [
                (start_in, start_ref),
                (gain_in, gain_ref),
                (bias_in, bias_ref),
                (readout_in, readout_ref),
                (conv_bias_in, conv_bias_ref),
                (conv_in_in, conv_in_ref),
                (conv_out_in, conv_out_ref),
                (interp_in, interp_ref),
                (pixel_in, pixel_ref),
                (det_in, det_ref),
                (count_in, count_ref),
                (measured_in, measured_ref),
            ]
        )
    ]
    for load in loads:
        load.start()
    halo[...] = jnp.zeros_like(halo)
    rows = 2 + 4 * REACH
    if slabs == 2:
        depth = 10 + layers
        base = slab * (8 - layers) - 1
        own = slab * layers + 1
    else:
        depth = 8 + 2 * layers
        base = 8 * slab - layers
        own = layers
    for ref in (taps_even, taps_odd):
        ref[0] = jnp.zeros(ref.shape[1:], BF16)
        ref[depth - 1] = jnp.zeros(ref.shape[1:], BF16)

    def prepare_weights():
        for layer in range(layers):
            for oz in range(3):
                stacked = jnp.concatenate(
                    [
                        conv_in_ref[layer, 9 * ox + 3 * oz + oy]
                        for ox in range(3)
                        for oy in range(3)
                    ],
                    axis=0,
                )
                weights[layer, channels * oz : channels * (oz + 1), :] = (
                    stacked.astype(F32).T.astype(BF16)
                )
            wide = jnp.concatenate([conv_out_ref[layer].astype(F32)] * 4, axis=1)
            place = lax.broadcasted_iota(jnp.int32, wide.shape, 1) // channels
            for k in range(4):
                weights_out[layer, half * k : half * (k + 1), :] = jnp.where(
                    place == k, wide, 0.0
                ).astype(BF16)
        vectors = [gain_ref[...], bias_ref[...], readout_ref[...]]
        vectors += [conv_bias_ref[layer : layer + 1, :] for layer in range(layers)]
        for index, vector in enumerate(vectors):
            columns_ref[channels * index : channels * (index + 1), :] = jnp.broadcast_to(
                vector, (128, channels)
            ).T

    barrier = pltpu.get_barrier_semaphore()
    partners(
        lambda other: pl.semaphore_signal(
            barrier, inc=1, device_id=device(other, slab), device_id_type=MESH
        )
    )
    greeted = group - 1
    for ds, dg in offsets:
        if ds == 0:
            continue

        def greet(ds=ds, dg=dg):
            pl.semaphore_signal(
                barrier, inc=1, device_id=device(me + dg, slab + ds), device_id_type=MESH
            )

        pl.when(present(ds, dg))(greet)
        greeted = greeted + present(ds, dg).astype(jnp.int32)
    for load in loads[:7]:
        load.wait()
    prepare_weights()
    pl.semaphore_wait(barrier, greeted)

    def gather_copy(turn, other, owner):
        return pltpu.make_async_remote_copy(
            src_ref=volume.at[turn, me],
            dst_ref=volume.at[turn, owner],
            send_sem=gather_send.at[turn, other],
            recv_sem=gather_recv.at[turn, owner],
            device_id=device(other, slab),
            device_id_type=MESH,
        )

    def gather_start(turn, block):
        volume[turn, me] = block.astype(BF16)
        partners(lambda other: gather_copy(turn, other, me).start())

    def gather_wait(turn):
        def wait(other):
            gather_copy(turn, other, other).wait_recv()
            gather_copy(turn, other, other).wait_send()

        partners(wait)

    def sum_copy(turn, other, owner):
        return pltpu.make_async_remote_copy(
            src_ref=partial.at[turn, other],
            dst_ref=arrived.at[turn, owner],
            send_sem=sum_send.at[turn, other],
            recv_sem=sum_recv.at[turn, owner],
            device_id=device(other, slab),
            device_id_type=MESH,
        )

    def sum_finish(turn):
        def step(k, total):
            other = lax.rem(me + k, group)
            sum_copy(turn, other, other).wait_recv()
            sum_copy(turn, other, other).wait_send()
            return total + arrived[turn, other].astype(F32)

        return lax.fori_loop(1, group, step, partial[turn, me].astype(F32))

    def halo_copy(turn, ds, dg, send):
        place = (1 - ds) * (2 * REACH + 1) + REACH - dg
        if not send:
            place = (1 + ds) * (2 * REACH + 1) + REACH + dg
        sent_place = (1 + ds) * (2 * REACH + 1) + REACH + dg
        return pltpu.make_async_remote_copy(
            src_ref=halo.at[turn, 3 * REACH + 1],
            dst_ref=halo.at[turn, place],
            send_sem=halo_send.at[turn, sent_place],
            recv_sem=halo_recv.at[turn, place],
            device_id=device(me + dg, slab + ds),
            device_id_type=MESH,
        )

    def halo_start(turn, block):
        halo[turn, 3 * REACH + 1] = block
        neighbours(lambda ds, dg: halo_copy(turn, ds, dg, True).start())

    def halo_wait(turn):
        def wait(ds, dg):
            halo_copy(turn, ds, dg, False).wait_recv()
            halo_copy(turn, ds, dg, False).wait_send()

        neighbours(wait)

    def data_step(turn):
        def widen(member, carry):
            volume_rows[pl.ds(2 * member, 2)] = (
                volume[turn, member].astype(F32).reshape(2, 8, 128)
            )
            return carry

        lax.fori_loop(0, group, widen, 0)
        live = [(count_ref[0, 0] > s).astype(F32) for s in range(slots)]
        first = [
            jnp.where(det_ref[0, s] == 0, F32(1.0), F32(0.0)) * live[s] for s in range(slots)
        ]
        second = [
            jnp.where(det_ref[0, s] == 1, F32(1.0), F32(0.0)) * live[s] for s in range(slots)
        ]
        for s in range(slots):
            row = volume_rows[pixel_ref[0, s]]
            lhs[:, 128 * s : 128 * (s + 1)] = jnp.concatenate(
                [row * first[s], row * second[s]], axis=0
            ).astype(BF16)
        projected = jnp.dot(lhs[...], interp_ref[...], preferred_element_type=F32)
        misfit = (projected - measured_ref[...]).astype(BF16)
        for s in range(0, slots, 2):
            both = lax.dot_general(
                misfit,
                interp_ref[128 * s : 128 * (s + 2), :],
                (((1,), (1,)), ((), ())),
                preferred_element_type=F32,
            )
            for k in range(2):
                block = both[:, 128 * k : 128 * (k + 1)]
                smeared[s + k] = block[:8] * first[s + k] + block[8:] * second[s + k]

        def rows_of(owner, carry):
            totals = [jnp.zeros((8, 128), F32) for _ in range(8)]
            for s in range(slots):
                at = jnp.full((8, 128), pixel_ref[0, s], jnp.int32) - 8 * owner
                block = smeared[s]
                for k in range(8):
                    totals[k] = totals[k] + jnp.where(at == k, block, 0.0)
            for k in range(4):
                partial[turn, 4 * owner + k] = jnp.concatenate(
                    totals[2 * k : 2 * k + 2], axis=0
                ).astype(BF16)
            return carry

        lax.fori_loop(0, group // 4, rows_of, 0)
        partners(lambda other: sum_copy(turn, other, me).start())

    def column(index):
        return columns_ref[channels * index : channels * (index + 1), :]

    lanes = lax.broadcasted_iota(jnp.int32, (half, 128), 1)

    def inside(i, j):
        row = 2 * me - 2 * REACH + i
        within = jnp.logical_and(row >= 0, row < 2 * group)
        if slabs != 2:
            at = base + j
            within = jnp.logical_and(within, jnp.logical_and(at >= 0, at < 8 * slabs))
        return within.astype(F32)

    def put_taps(target, i, j, block):
        block = block * inside(i, j)
        before = jnp.where(lanes == 0, 0.0, pltpu.roll(block, 1, 1))
        after = jnp.where(lanes == 127, 0.0, pltpu.roll(block, 127, 1))
        target[j, i] = jnp.concatenate([before, block, after], axis=0).astype(BF16)

    def denoise(turn, between):
        gain, bias = column(0), column(1)

        def lift(i, carry):
            block, low = i // 2, 8 * lax.rem(i, 2)
            above = halo[turn, block, pl.ds(pl.multiple_of(low, 8), 8), :]
            here = halo[turn, 2 * REACH + 1 + block, pl.ds(pl.multiple_of(low, 8), 8), :]
            below = halo[turn, 4 * REACH + 2 + block, pl.ds(pl.multiple_of(low, 8), 8), :]
            if slabs == 2:
                line = jnp.where(
                    slab == 0,
                    jnp.concatenate([here, below[:layers]], axis=0),
                    jnp.concatenate([above[8 - layers :], here], axis=0),
                )
                first = 1
            else:
                line = jnp.concatenate([above[8 - layers :], here, below[:layers]], axis=0)
                first = 0
            for j in range(line.shape[0]):
                block = gain * line[j : j + 1, :] + bias
                features[i, first + j] = block
                put_taps(taps_even, i, first + j, block[:half])
            return carry

        lax.fori_loop(0, rows, lift, 0)

        for layer in range(layers):
            passive = half if layer % 2 == 0 else 0
            taps, taps_next = (
                (taps_even, taps_odd) if layer % 2 == 0 else (taps_odd, taps_even)
            )
            bias_wide = jnp.concatenate([column(3 + layer)] * 2, axis=1)
            pairs = rows // 2 - 1 - layer
            if slabs == 2:
                low, count = 1 + slab * (1 + layer), 7 + layers - layer
            else:
                low, count = 1 + layer, 6 + 2 * layers - 2 * layer
            unroll = min(u for u in range(1, count + 1) if count % u == 0 and u * pairs >= 4)

            def multiply(p, j):
                r = layer + 1 + 2 * p
                left = taps[j, r - 1 : r + 2].reshape(9 * half, 128)
                right = taps[j, r : r + 3].reshape(9 * half, 128)
                products[p, j] = jnp.dot(
                    weights[layer],
                    jnp.concatenate([left, right], axis=1),
                    preferred_element_type=F32,
                )

            def activate(p, j):
                total = (
                    products[p, j - 1, :channels]
                    + products[p, j, channels : 2 * channels]
                    + products[p, j + 1, 2 * channels :]
                    + bias_wide
                )
                return (total / (1.0 + jnp.exp(-total))).astype(BF16)

            def add(p, j, change):
                r = layer + 1 + 2 * p
                for k in range(2):
                    block = (
                        features[r + k, j, passive : passive + half, :]
                        + change[:, 128 * k : 128 * (k + 1)]
                    )
                    features[r + k, j, passive : passive + half, :] = block
                    if layer + 1 < layers:
                        put_taps(taps_next, r + k, j, block)

            def several(j, number):
                return [(p, j + k) for k in range(number) for p in range(pairs)]

            def finish(j):
                items = several(j, unroll)
                for at in range(0, len(items), 4):
                    some = items[at : at + 4]
                    inner = jnp.concatenate([activate(*item) for item in some], axis=0)
                    change = jnp.dot(
                        weights_out[layer, : half * len(some), : channels * len(some)],
                        inner,
                        preferred_element_type=F32,
                    )
                    for k, item in enumerate(some):
                        add(*item, change[half * k : half * (k + 1)])

            def begin(t, carry):
                for item in several(low - 1 + t, 1):
                    multiply(*item)
                return carry

            def along(t, carry):
                finish(low + unroll * t)
                for item in several(low + 1 + unroll * (t + 1), unroll):
                    multiply(*item)
                return carry

            lax.fori_loop(0, unroll + 2, begin, 0)
            lax.fori_loop(0, count // unroll - 1, along, 0)
            finish(low + count - unroll)
            if layer == 0:
                between()

        readout = column(2)
        lines = []
        for i in range(2):
            for j in range(8):
                lines.append(
                    jnp.sum(features[2 * REACH + i, own + j] * readout, axis=0, keepdims=True)
                )
        return halo[turn, 3 * REACH + 1] + jnp.concatenate(lines, axis=0)

    estimate = start_ref[...]
    denoised = estimate
    scaled_dual = jnp.zeros_like(estimate)
    gather_start(0, estimate)
    gather_wait(0)
    for load in loads[7:]:
        load.wait()
    data_step(0)
    for turn in range(ITERS):
        gradient = sum_finish(turn)
        estimate = estimate - STEP * (gradient + RHO * (estimate - denoised + scaled_dual))
        if turn + 1 == ITERS:
            estimate_ref[...] = estimate
        halo_start(turn, estimate + scaled_dual)
        if turn + 1 < ITERS:
            gather_start(turn + 1, estimate)
        halo_wait(turn)

        def between(turn=turn):
            if turn + 1 < ITERS:
                gather_wait(turn + 1)
                data_step(turn + 1)

        fresh = denoise(turn, between)
        if turn + 1 < ITERS:
            scaled_dual = scaled_dual + estimate - fresh
        denoised = fresh
    denoised_ref[...] = denoised


def solution(mesh):
    in_specs = (
        P("angle", "tile", ("parts", "slab"), None),
        P(("angle", "tile"), ("parts", "slab"), None),
        P("angle", "tile"),
        P("angle", "tile"),
        P("angle", "tile"),
        P("angle", "tile", None, None),
        P(),
        P(),
        P(),
        P(),
        P(),
        P(),
    )
    out_specs = (
        P(("angle", "tile"), ("parts", "slab"), None),
        P(("angle", "tile"), ("parts", "slab"), None),
    )
    tiles = mesh.shape["tile"]
    group = mesh.shape["angle"] * tiles
    slabs = mesh.shape["slab"]

    def local(
        measured,
        x_start,
        block_pixel,
        block_det,
        block_count,
        interp,
        lift_gain,
        lift_bias,
        conv_in,
        conv_bias,
        conv_out,
        out_gain,
    ):
        channels = lift_gain.shape[0]
        layers = conv_in.shape[0]
        slots = interp.shape[1]
        half = channels // 2
        rows = 2 + 4 * REACH
        depth = 10 + layers if slabs == 2 else 8 + 2 * layers
        vmem = pl.BlockSpec(memory_space=pltpu.VMEM)
        hbm = pl.BlockSpec(memory_space=pltpu.HBM)
        places = 3 * (2 * REACH + 1)

        def run(*refs):
            kernel(group, tiles, slabs, layers, channels, *refs)

        estimate, denoised = pl.pallas_call(
            run,
            out_shape=[jax.ShapeDtypeStruct((16, 128), F32)] * 2,
            in_specs=[hbm] * 12,
            out_specs=[vmem] * 2,
            scratch_shapes=[
                pltpu.SMEM(block_pixel.shape, jnp.int32),
                pltpu.SMEM(block_det.shape, jnp.int32),
                pltpu.SMEM(block_count.shape, jnp.int32),
                pltpu.VMEM((16, 128), F32),
                pltpu.VMEM((16, 128), F32),
                pltpu.VMEM((slots * 128, 128), BF16),
                pltpu.VMEM(conv_in.shape, BF16),
                pltpu.VMEM((layers, half, channels), BF16),
                pltpu.VMEM((1, channels), F32),
                pltpu.VMEM((1, channels), F32),
                pltpu.VMEM((1, channels), F32),
                pltpu.VMEM((layers, channels), F32),
                pltpu.VMEM(((3 + layers) * channels, 128), F32),
                pltpu.VMEM((ITERS, group, 16, 128), BF16),
                pltpu.VMEM((2 * group, 8, 128), F32),
                pltpu.VMEM((16, 128 * slots), BF16),
                pltpu.VMEM((slots, 8, 128), F32),
                pltpu.VMEM((ITERS, group, 16, 128), BF16),
                pltpu.VMEM((ITERS, group, 16, 128), BF16),
                pltpu.VMEM((ITERS, places, 16, 128), F32),
                pltpu.VMEM((layers, 3 * channels, 9 * half), BF16),
                pltpu.VMEM((layers, 4 * half, 4 * channels), BF16),
                pltpu.VMEM((rows, depth, channels, 128), F32),
                pltpu.VMEM((depth, rows, 3 * half, 128), BF16),
                pltpu.VMEM((depth, rows, 3 * half, 128), BF16),
                pltpu.VMEM((rows // 2 - 1, depth, 3 * channels, 256), F32),
                pltpu.SemaphoreType.DMA((12,)),
                pltpu.SemaphoreType.DMA((ITERS, group)),
                pltpu.SemaphoreType.DMA((ITERS, group)),
                pltpu.SemaphoreType.DMA((ITERS, group)),
                pltpu.SemaphoreType.DMA((ITERS, group)),
                pltpu.SemaphoreType.DMA((ITERS, places)),
                pltpu.SemaphoreType.DMA((ITERS, places)),
            ],
            compiler_params=pltpu.CompilerParams(
                collective_id=0, has_side_effects=True, vmem_limit_bytes=48 * 1024 * 1024
            ),
        )(
            block_pixel,
            block_det,
            block_count,
            x_start.reshape(16, 128),
            measured.reshape(16, 128),
            interp.reshape(slots * 128, 128),
            conv_in,
            jnp.swapaxes(conv_out, 1, 2),
            lift_gain.reshape(1, channels),
            lift_bias.reshape(1, channels),
            out_gain.reshape(1, channels),
            conv_bias,
        )
        return estimate.reshape(2, 8, 128), denoised.reshape(2, 8, 128)

    return jax.shard_map(local, mesh=mesh, in_specs=in_specs, out_specs=out_specs, check_vma=False)
```

```python
import jax
import jax.numpy as jnp
from jax import lax
from jax.experimental import pallas as pl
from jax.experimental.pallas import tpu as pltpu
from jax.sharding import PartitionSpec as P

ITERS = 2
STEP = 0.2
RHO = 0.5
REACH = 2
F32 = jnp.float32
BF16 = jnp.bfloat16
MESH = pl.DeviceIdType.MESH


def kernel(
    group,
    tiles,
    slabs,
    layers,
    channels,
    pixel_in,
    det_in,
    count_in,
    start_in,
    measured_in,
    interp_in,
    conv_in_in,
    conv_out_in,
    gain_in,
    bias_in,
    readout_in,
    conv_bias_in,
    estimate_ref,
    denoised_ref,
    pixel_ref,
    det_ref,
    count_ref,
    start_ref,
    measured_ref,
    interp_ref,
    conv_in_ref,
    conv_out_ref,
    gain_ref,
    bias_ref,
    readout_ref,
    conv_bias_ref,
    columns_ref,
    volume,
    volume_rows,
    lhs,
    smeared,
    partial,
    arrived,
    halo,
    weights,
    weights_out,
    features,
    taps_even,
    taps_odd,
    products,
    input_sems,
    gather_send,
    gather_recv,
    sum_send,
    sum_recv,
    halo_send,
    halo_recv,
):
    half = channels // 2
    part = lax.axis_index("parts")
    slab = lax.axis_index("slab")
    me = lax.axis_index("angle") * tiles + lax.axis_index("tile")
    slots = interp_ref.shape[0] // 128

    def device(member, at_slab):
        return (part, member // tiles, at_slab, lax.rem(member, tiles))

    offsets = [
        (ds, dg) for ds in (-1, 0, 1) for dg in range(-REACH, REACH + 1) if (ds, dg) != (0, 0)
    ]

    def present(ds, dg):
        return jnp.logical_and(
            jnp.logical_and(me + dg >= 0, me + dg < group),
            jnp.logical_and(slab + ds >= 0, slab + ds < slabs),
        )

    def partners(body):
        def step(k, carry):
            body(lax.rem(me + k, group))
            return carry

        lax.fori_loop(1, group, step, 0, unroll=group <= 8)

    def neighbours(body):
        for ds, dg in offsets:
            pl.when(present(ds, dg))(lambda ds=ds, dg=dg: body(ds, dg))

    loads = [
        pltpu.make_async_copy(source, target, input_sems.at[index])
        for index, (source, target) in enumerate(
            [
                (start_in, start_ref),
                (gain_in, gain_ref),
                (bias_in, bias_ref),
                (readout_in, readout_ref),
                (conv_bias_in, conv_bias_ref),
                (conv_in_in, conv_in_ref),
                (conv_out_in, conv_out_ref),
                (interp_in, interp_ref),
                (pixel_in, pixel_ref),
                (det_in, det_ref),
                (count_in, count_ref),
                (measured_in, measured_ref),
            ]
        )
    ]
    for load in loads:
        load.start()
    halo[...] = jnp.zeros_like(halo)
    rows = 2 + 4 * REACH
    if slabs == 2:
        depth = 10 + layers
        base = slab * (8 - layers) - 1
        own = slab * layers + 1
    else:
        depth = 8 + 2 * layers
        base = 8 * slab - layers
        own = layers
    for ref in (taps_even, taps_odd):
        ref[0] = jnp.zeros(ref.shape[1:], BF16)
        ref[depth - 1] = jnp.zeros(ref.shape[1:], BF16)

    def prepare_weights():
        for layer in range(layers):
            for oz in range(3):
                stacked = jnp.concatenate(
                    [
                        conv_in_ref[layer, 9 * ox + 3 * oz + oy]
                        for ox in range(3)
                        for oy in range(3)
                    ],
                    axis=0,
                )
                weights[layer, channels * oz : channels * (oz + 1), :] = (
                    stacked.astype(F32).T.astype(BF16)
                )
            wide = jnp.concatenate([conv_out_ref[layer].astype(F32)] * 4, axis=1)
            place = lax.broadcasted_iota(jnp.int32, wide.shape, 1) // channels
            for k in range(4):
                weights_out[layer, half * k : half * (k + 1), :] = jnp.where(
                    place == k, wide, 0.0
                ).astype(BF16)
        vectors = [gain_ref[...], bias_ref[...], readout_ref[...]]
        vectors += [conv_bias_ref[layer : layer + 1, :] for layer in range(layers)]
        for index, vector in enumerate(vectors):
            columns_ref[channels * index : channels * (index + 1), :] = jnp.broadcast_to(
                vector, (128, channels)
            ).T

    barrier = pltpu.get_barrier_semaphore()
    partners(
        lambda other: pl.semaphore_signal(
            barrier, inc=1, device_id=device(other, slab), device_id_type=MESH
        )
    )
    greeted = group - 1
    for ds, dg in offsets:
        if ds == 0:
            continue

        def greet(ds=ds, dg=dg):
            pl.semaphore_signal(
                barrier, inc=1, device_id=device(me + dg, slab + ds), device_id_type=MESH
            )

        pl.when(present(ds, dg))(greet)
        greeted = greeted + present(ds, dg).astype(jnp.int32)
    for load in loads[:7]:
        load.wait()
    prepare_weights()
    pl.semaphore_wait(barrier, greeted)

    def gather_copy(turn, other, owner):
        return pltpu.make_async_remote_copy(
            src_ref=volume.at[turn, me],
            dst_ref=volume.at[turn, owner],
            send_sem=gather_send.at[turn, other],
            recv_sem=gather_recv.at[turn, owner],
            device_id=device(other, slab),
            device_id_type=MESH,
        )

    def gather_start(turn, block):
        volume[turn, me] = block.astype(BF16)
        partners(lambda other: gather_copy(turn, other, me).start())

    def gather_wait(turn):
        def wait(other):
            gather_copy(turn, other, other).wait_recv()

        partners(wait)

    def sum_copy(turn, other, owner):
        return pltpu.make_async_remote_copy(
            src_ref=partial.at[turn, other],
            dst_ref=arrived.at[turn, owner],
            send_sem=sum_send.at[turn, other],
            recv_sem=sum_recv.at[turn, owner],
            device_id=device(other, slab),
            device_id_type=MESH,
        )

    def sum_finish(turn):
        def step(k, total):
            other = lax.rem(me + k, group)
            sum_copy(turn, other, other).wait_recv()
            return total + arrived[turn, other].astype(F32)

        return lax.fori_loop(1, group, step, partial[turn, me].astype(F32), unroll=group <= 8)

    def halo_copy(turn, ds, dg, send):
        place = (1 - ds) * (2 * REACH + 1) + REACH - dg
        if not send:
            place = (1 + ds) * (2 * REACH + 1) + REACH + dg
        sent_place = (1 + ds) * (2 * REACH + 1) + REACH + dg
        return pltpu.make_async_remote_copy(
            src_ref=halo.at[turn, 3 * REACH + 1],
            dst_ref=halo.at[turn, place],
            send_sem=halo_send.at[turn, sent_place],
            recv_sem=halo_recv.at[turn, place],
            device_id=device(me + dg, slab + ds),
            device_id_type=MESH,
        )

    def halo_start(turn, block):
        halo[turn, 3 * REACH + 1] = block
        neighbours(lambda ds, dg: halo_copy(turn, ds, dg, True).start())

    def halo_wait(turn):
        def wait(ds, dg):
            halo_copy(turn, ds, dg, False).wait_recv()

        neighbours(wait)

    def sends_wait(turn):
        def wait(other):
            gather_copy(turn, other, other).wait_send()
            sum_copy(turn, other, other).wait_send()

        partners(wait)
        neighbours(lambda ds, dg: halo_copy(turn, ds, dg, False).wait_send())

    def data_step(turn):
        def widen(member, carry):
            volume_rows[pl.ds(2 * member, 2)] = (
                volume[turn, member].astype(F32).reshape(2, 8, 128)
            )
            return carry

        lax.fori_loop(0, group, widen, 0)
        live = [(count_ref[0, 0] > s).astype(F32) for s in range(slots)]
        first = [
            jnp.where(det_ref[0, s] == 0, F32(1.0), F32(0.0)) * live[s] for s in range(slots)
        ]
        second = [
            jnp.where(det_ref[0, s] == 1, F32(1.0), F32(0.0)) * live[s] for s in range(slots)
        ]
        for s in range(slots):
            row = volume_rows[pixel_ref[0, s]]
            lhs[:, 128 * s : 128 * (s + 1)] = jnp.concatenate(
                [row * first[s], row * second[s]], axis=0
            ).astype(BF16)
        projected = jnp.dot(lhs[...], interp_ref[...], preferred_element_type=F32)
        misfit = (projected - measured_ref[...]).astype(BF16)
        for s in range(0, slots, 2):
            both = lax.dot_general(
                misfit,
                interp_ref[128 * s : 128 * (s + 2), :],
                (((1,), (1,)), ((), ())),
                preferred_element_type=F32,
            )
            for k in range(2):
                block = both[:, 128 * k : 128 * (k + 1)]
                smeared[s + k] = block[:8] * first[s + k] + block[8:] * second[s + k]

        def rows_of(owner, carry):
            totals = [jnp.zeros((8, 128), F32) for _ in range(8)]
            for s in range(slots):
                at = jnp.full((8, 128), pixel_ref[0, s], jnp.int32) - 8 * owner
                block = smeared[s]
                for k in range(8):
                    totals[k] = totals[k] + jnp.where(at == k, block, 0.0)
            for k in range(4):
                partial[turn, 4 * owner + k] = jnp.concatenate(
                    totals[2 * k : 2 * k + 2], axis=0
                ).astype(BF16)
            return carry

        lax.fori_loop(0, group // 4, rows_of, 0)
        partners(lambda other: sum_copy(turn, other, me).start())

    def column(index):
        return columns_ref[channels * index : channels * (index + 1), :]

    lanes = lax.broadcasted_iota(jnp.int32, (half, 128), 1)

    def inside(i, j):
        row = 2 * me - 2 * REACH + i
        within = jnp.logical_and(row >= 0, row < 2 * group)
        if slabs != 2:
            at = base + j
            within = jnp.logical_and(within, jnp.logical_and(at >= 0, at < 8 * slabs))
        return within.astype(F32)

    def put_taps(target, i, j, block):
        block = block * inside(i, j)
        before = jnp.where(lanes == 0, 0.0, pltpu.roll(block, 1, 1))
        after = jnp.where(lanes == 127, 0.0, pltpu.roll(block, 127, 1))
        target[j, i] = jnp.concatenate([before, block, after], axis=0).astype(BF16)

    def denoise(turn, between):
        gain, bias = column(0), column(1)

        def lift(i, carry):
            block, low = i // 2, 8 * lax.rem(i, 2)
            above = halo[turn, block, pl.ds(pl.multiple_of(low, 8), 8), :]
            here = halo[turn, 2 * REACH + 1 + block, pl.ds(pl.multiple_of(low, 8), 8), :]
            below = halo[turn, 4 * REACH + 2 + block, pl.ds(pl.multiple_of(low, 8), 8), :]
            if slabs == 2:
                line = jnp.where(
                    slab == 0,
                    jnp.concatenate([here, below[:layers]], axis=0),
                    jnp.concatenate([above[8 - layers :], here], axis=0),
                )
                first = 1
            else:
                line = jnp.concatenate([above[8 - layers :], here, below[:layers]], axis=0)
                first = 0
            for j in range(line.shape[0]):
                block = gain * line[j : j + 1, :] + bias
                features[i, first + j] = block
                put_taps(taps_even, i, first + j, block[:half])
            return carry

        lax.fori_loop(0, rows, lift, 0)

        for layer in range(layers):
            passive = half if layer % 2 == 0 else 0
            taps, taps_next = (
                (taps_even, taps_odd) if layer % 2 == 0 else (taps_odd, taps_even)
            )
            bias_wide = jnp.concatenate([column(3 + layer)] * 2, axis=1)
            pairs = rows // 2 - 1 - layer
            if slabs == 2:
                low, count = 1 + slab * (1 + layer), 7 + layers - layer
            else:
                low, count = 1 + layer, 6 + 2 * layers - 2 * layer
            unroll = min(u for u in range(1, count + 1) if count % u == 0 and u * pairs >= 4)

            def multiply(p, j):
                r = layer + 1 + 2 * p
                left = taps[j, r - 1 : r + 2].reshape(9 * half, 128)
                right = taps[j, r : r + 3].reshape(9 * half, 128)
                products[p, j] = jnp.dot(
                    weights[layer],
                    jnp.concatenate([left, right], axis=1),
                    preferred_element_type=F32,
                )

            def activate(p, j):
                total = (
                    products[p, j - 1, :channels]
                    + products[p, j, channels : 2 * channels]
                    + products[p, j + 1, 2 * channels :]
                    + bias_wide
                )
                total = 0.5 * total
                return (total + total * jnp.tanh(total)).astype(BF16)

            def add(p, j, change):
                r = layer + 1 + 2 * p
                for k in range(2):
                    block = (
                        features[r + k, j, passive : passive + half, :]
                        + change[:, 128 * k : 128 * (k + 1)]
                    )
                    features[r + k, j, passive : passive + half, :] = block
                    if layer + 1 < layers:
                        put_taps(taps_next, r + k, j, block)

            def several(j, number):
                return [(p, j + k) for k in range(number) for p in range(pairs)]

            def finish(j):
                items = several(j, unroll)
                for at in range(0, len(items), 4):
                    some = items[at : at + 4]
                    inner = jnp.concatenate([activate(*item) for item in some], axis=0)
                    change = jnp.dot(
                        weights_out[layer, : half * len(some), : channels * len(some)],
                        inner,
                        preferred_element_type=F32,
                    )
                    for k, item in enumerate(some):
                        add(*item, change[half * k : half * (k + 1)])

            def begin(t, carry):
                for item in several(low - 1 + t, 1):
                    multiply(*item)
                return carry

            def along(t, carry):
                finish(low + unroll * t)
                for item in several(low + 1 + unroll * (t + 1), unroll):
                    multiply(*item)
                return carry

            lax.fori_loop(0, unroll + 2, begin, 0)
            lax.fori_loop(0, count // unroll - 1, along, 0)
            finish(low + count - unroll)
            if layer == 0:
                between()

        readout = column(2)
        lines = []
        for i in range(2):
            for j in range(8):
                lines.append(
                    jnp.sum(features[2 * REACH + i, own + j] * readout, axis=0, keepdims=True)
                )
        return halo[turn, 3 * REACH + 1] + jnp.concatenate(lines, axis=0)

    estimate = start_ref[...]
    denoised = estimate
    scaled_dual = jnp.zeros_like(estimate)
    gather_start(0, estimate)
    gather_wait(0)
    for load in loads[7:]:
        load.wait()
    data_step(0)
    for turn in range(ITERS):
        gradient = sum_finish(turn)
        estimate = estimate - STEP * (gradient + RHO * (estimate - denoised + scaled_dual))
        if turn + 1 == ITERS:
            estimate_ref[...] = estimate
        halo_start(turn, estimate + scaled_dual)
        if turn + 1 < ITERS:
            gather_start(turn + 1, estimate)
        halo_wait(turn)

        def between(turn=turn):
            if turn + 1 < ITERS:
                gather_wait(turn + 1)
                data_step(turn + 1)

        fresh = denoise(turn, between)
        if turn + 1 < ITERS:
            scaled_dual = scaled_dual + estimate - fresh
        denoised = fresh
    denoised_ref[...] = denoised
    for turn in range(ITERS):
        sends_wait(turn)


def solution(mesh):
    in_specs = (
        P("angle", "tile", ("parts", "slab"), None),
        P(("angle", "tile"), ("parts", "slab"), None),
        P("angle", "tile"),
        P("angle", "tile"),
        P("angle", "tile"),
        P("angle", "tile", None, None),
        P(),
        P(),
        P(),
        P(),
        P(),
        P(),
    )
    out_specs = (
        P(("angle", "tile"), ("parts", "slab"), None),
        P(("angle", "tile"), ("parts", "slab"), None),
    )
    tiles = mesh.shape["tile"]
    group = mesh.shape["angle"] * tiles
    slabs = mesh.shape["slab"]

    def local(
        measured,
        x_start,
        block_pixel,
        block_det,
        block_count,
        interp,
        lift_gain,
        lift_bias,
        conv_in,
        conv_bias,
        conv_out,
        out_gain,
    ):
        channels = lift_gain.shape[0]
        layers = conv_in.shape[0]
        slots = interp.shape[1]
        half = channels // 2
        rows = 2 + 4 * REACH
        depth = 10 + layers if slabs == 2 else 8 + 2 * layers
        vmem = pl.BlockSpec(memory_space=pltpu.VMEM)
        hbm = pl.BlockSpec(memory_space=pltpu.HBM)
        places = 3 * (2 * REACH + 1)

        def run(*refs):
            kernel(group, tiles, slabs, layers, channels, *refs)

        estimate, denoised = pl.pallas_call(
            run,
            out_shape=[jax.ShapeDtypeStruct((16, 128), F32)] * 2,
            in_specs=[hbm] * 12,
            out_specs=[vmem] * 2,
            scratch_shapes=[
                pltpu.SMEM(block_pixel.shape, jnp.int32),
                pltpu.SMEM(block_det.shape, jnp.int32),
                pltpu.SMEM(block_count.shape, jnp.int32),
                pltpu.VMEM((16, 128), F32),
                pltpu.VMEM((16, 128), F32),
                pltpu.VMEM((slots * 128, 128), BF16),
                pltpu.VMEM(conv_in.shape, BF16),
                pltpu.VMEM((layers, half, channels), BF16),
                pltpu.VMEM((1, channels), F32),
                pltpu.VMEM((1, channels), F32),
                pltpu.VMEM((1, channels), F32),
                pltpu.VMEM((layers, channels), F32),
                pltpu.VMEM(((3 + layers) * channels, 128), F32),
                pltpu.VMEM((ITERS, group, 16, 128), BF16),
                pltpu.VMEM((2 * group, 8, 128), F32),
                pltpu.VMEM((16, 128 * slots), BF16),
                pltpu.VMEM((slots, 8, 128), F32),
                pltpu.VMEM((ITERS, group, 16, 128), BF16),
                pltpu.VMEM((ITERS, group, 16, 128), BF16),
                pltpu.VMEM((ITERS, places, 16, 128), F32),
                pltpu.VMEM((layers, 3 * channels, 9 * half), BF16),
                pltpu.VMEM((layers, 4 * half, 4 * channels), BF16),
                pltpu.VMEM((rows, depth, channels, 128), F32),
                pltpu.VMEM((depth, rows, 3 * half, 128), BF16),
                pltpu.VMEM((depth, rows, 3 * half, 128), BF16),
                pltpu.VMEM((rows // 2 - 1, depth, 3 * channels, 256), F32),
                pltpu.SemaphoreType.DMA((12,)),
                pltpu.SemaphoreType.DMA((ITERS, group)),
                pltpu.SemaphoreType.DMA((ITERS, group)),
                pltpu.SemaphoreType.DMA((ITERS, group)),
                pltpu.SemaphoreType.DMA((ITERS, group)),
                pltpu.SemaphoreType.DMA((ITERS, places)),
                pltpu.SemaphoreType.DMA((ITERS, places)),
            ],
            compiler_params=pltpu.CompilerParams(
                collective_id=0, has_side_effects=True, vmem_limit_bytes=63 * 1024 * 1024
            ),
        )(
            block_pixel,
            block_det,
            block_count,
            x_start.reshape(16, 128),
            measured.reshape(16, 128),
            interp.reshape(slots * 128, 128),
            conv_in,
            jnp.swapaxes(conv_out, 1, 2),
            lift_gain.reshape(1, channels),
            lift_bias.reshape(1, channels),
            out_gain.reshape(1, channels),
            conv_bias,
        )
        return estimate.reshape(2, 8, 128), denoised.reshape(2, 8, 128)

    return jax.shard_map(local, mesh=mesh, in_specs=in_specs, out_specs=out_specs, check_vma=False)
```
